32 devices in a mesh: groups: 2 (over x), blk: 4 (over y, core), tok: 4 (over z).
Axes of the slice: x: 2, y: 2, z: 4, core: 2. Of those that a mesh axis runs over, the one named last changes fastest.
Arguments:
- latent_codes: bfloat16 [512, 2, 16, 512], P(('groups', 'tok'), None, 'blk'), parts along dimension 0, may hold values from 0.049804688 to 0.5
- block_lists: int32 [16, 2, 16, 8], P('groups', None, 'blk'), parts along dimension 0, may hold values from 0 to 15, as said below
- block_counts: int32 [16, 2, 16], P('groups', None, 'blk'), parts along dimension 0, may hold values from 1 to 8, as said below
- decoder: bfloat16 [3, 16384, 8192], P(None, 'blk', 'tok'), may hold values from -0.29882812 to 0.29882812
- targets: bfloat16 [512, 2, 8192], P(('groups', 'blk'), None, 'tok'), parts along dimension 0, may hold values from -6 to 6
Outputs:
- recon_error: bfloat16 [512, 2, 8192], P(('groups', 'blk'), None, 'tok'), parts along dimension 0
- decoder_grad: bfloat16 [6, 16384, 8192], P('groups', 'blk', 'tok'), parts along dimension 0
- code_grad: bfloat16 [512, 2, 16, 512], P(('groups', 'tok'), None, 'blk'), parts along dimension 0
The draws below stay inside these ranges and needn't reach their ends.
There are 2 independent parts, one for each index of `groups`. The reference program is written for one: setup_inputs(seed, part) draws one part's arguments, and reference() takes and returns one part's arrays. A program takes and returns all parts, laid end to end along the dimension named above; an argument that names none is the same for every part. Nothing has to cross between parts.
Inputs may be any that keep to these rules, and one draw needn't show every extreme that they name: `block_lists`: within one tile, source layer and region the 8 listed block numbers are distinct; only the first block_counts of them are active, the others are ignored. `block_counts`: 8 is reached in every draw.
All inputs are finite; a program needn't handle non-finite values.
Results may differ from the reference program's by a relative error of at most 0.014.
Values may be sent and summed in bfloat16 or wider, within the bound.
A program may use at most 320 MiB of HBM per device.

```python
import math
import jax
import jax.numpy as jnp
from jax import lax

D = 8192
LAT = 16384
NREG = 16
BLOCK = 64
KR = 8
TILE = 32
L = 2
TOKENS = 256
TILES = 8
P_SIZE = 3
N_BLK = 4
N_TOK = 4


def draw_block_lists(key, part):
    key = jax.random.fold_in(key, 11)
    region_blocks = LAT // (NREG * BLOCK)
    scores = jax.random.randint(key, (TILES, L, NREG, region_blocks), 0, 1048576)
    keyed = scores * region_blocks + lax.broadcasted_iota(jnp.int32, (TILES, L, NREG, region_blocks), 3)
    order = jnp.argsort(keyed, axis=-1)
    return order[..., :KR].astype(jnp.int32)


def draw_block_counts(key, part):
    key = jax.random.fold_in(key, 23)
    drawn = jax.random.randint(key, (TILES, L, NREG), 1, KR + 1)
    drawn = drawn.at[0, 0, 0].set(KR)
    drawn = drawn.at[0, 0, 1].set(1)
    return drawn.astype(jnp.int32)


def level_of(key, dims, cuts, least, high):
    level, own = 1.0, jax.random.fold_in(key, 6)
    for position, blocks in cuts:
        heights = jnp.exp(jax.random.uniform(jax.random.fold_in(own, position), (blocks,), jnp.float32, least / len(cuts), high / len(cuts)))
        level = level * jnp.repeat(heights, dims[position] // blocks).reshape([-1 if axis == position else 1 for axis in range(len(dims))])
    return level


def gaussian(rng, shape, deviation, reach, cuts=(), dtype=jnp.bfloat16):
    loudness = level_of(rng, shape, cuts, -0.22, 0.18) if cuts else 1.0
    entries = jax.random.normal(rng, shape, jnp.float32) * deviation * loudness
    return jnp.minimum(jnp.maximum(entries, -reach), reach).astype(dtype)


def setup_inputs(seed: int = 0, part: int = 0) -> dict:
    arg_keys = jax.random.split(jax.random.key(seed), 6)
    part_splits = jax.random.split(jax.random.fold_in(arg_keys[5], part), 6)
    latent_codes = jnp.clip(jnp.exp(math.log(0.5) - 2.306499 * jax.random.uniform(part_splits[0], (TOKENS, L, NREG, KR * BLOCK), jnp.float32) ** level_of(part_splits[0], (TOKENS, L, NREG, KR * BLOCK), ((0, 4), (2, 4)), -0.2, 0.2)), 0.049804688, 0.5).astype(jnp.bfloat16)
    block_lists = draw_block_lists(jax.random.fold_in(jax.random.fold_in(arg_keys[5], part), 71), part)
    block_counts = draw_block_counts(jax.random.fold_in(jax.random.fold_in(arg_keys[5], part), 71), part)
    decoder = gaussian(arg_keys[3], (P_SIZE, LAT, D), 0.05, 0.29882812, ((1, 4), (2, 4)))
    targets = gaussian(part_splits[4], (TOKENS, L, D), 1.0, 6.0, ((0, 4), (2, 4)))
    return dict(latent_codes=latent_codes, block_lists=block_lists, block_counts=block_counts, decoder=decoder, targets=targets)


def pair_index(source, target):
    return source * L - source * (source - 1) // 2 + (target - source)


def selection(block_lists, block_counts, region_blocks):
    slot_index = lax.broadcasted_iota(jnp.int32, block_lists.shape, 3)
    active = slot_index < block_counts[..., None]
    block_ids = lax.broadcasted_iota(jnp.int32, block_lists.shape + (region_blocks,), 4)
    chosen = (block_lists[..., None] == block_ids) & active[..., None]
    return chosen.astype(jnp.float32)


def rounded(value):
    return lax.optimization_barrier(value.astype(jnp.bfloat16)).astype(jnp.float32)


def reference(latent_codes, block_lists, block_counts, decoder, targets):
    region_blocks = LAT // (NREG * BLOCK)
    select = selection(block_lists, block_counts, region_blocks)
    grouped = latent_codes.astype(jnp.float32).reshape(TILES, TILE, L, NREG, KR, BLOCK)
    spread = jnp.einsum("xtlrkc,xlrkb->xtlrbc", grouped, select)
    dense_codes = spread.reshape(TOKENS, L, LAT).astype(jnp.bfloat16)
    span = LAT // N_BLK
    per_target = []
    for target in range(L):
        total = jnp.zeros((TOKENS, D), jnp.float32)
        for group in range(N_BLK):
            running = jnp.zeros((TOKENS, D), jnp.float32)
            for source in range(target + 1):
                running = running + jnp.dot(dense_codes[:, source, group * span:(group + 1) * span], decoder[pair_index(source, target), group * span:(group + 1) * span], preferred_element_type=jnp.float32)
            total = total + rounded(running)
        per_target.append(total)
    rebuilt = jnp.stack(per_target, 1)
    recon_error = (rebuilt - targets.astype(jnp.float32)).astype(jnp.bfloat16)
    pair_grads = []
    for source in range(L):
        for target in range(source, L):
            product = lax.dot_general(dense_codes[:, source], recon_error[:, target], (((0,), (0,)), ((), ())), preferred_element_type=jnp.float32)
            pair_grads.append(product.astype(jnp.bfloat16))
    decoder_grad = jnp.stack(pair_grads, 0)
    width = D // N_TOK
    per_source = []
    for source in range(L):
        total = jnp.zeros((TOKENS, LAT), jnp.float32)
        for slice_index in range(N_TOK):
            running = jnp.zeros((TOKENS, LAT), jnp.float32)
            for target in range(source, L):
                running = running + lax.dot_general(recon_error[:, target, slice_index * width:(slice_index + 1) * width], decoder[pair_index(source, target), :, slice_index * width:(slice_index + 1) * width], (((1,), (1,)), ((), ())), preferred_element_type=jnp.float32)
            total = total + rounded(running)
        per_source.append(total)
    latent_grads = jnp.stack(per_source, 1).reshape(TILES, TILE, L, NREG, region_blocks, BLOCK)
    packed = jnp.einsum("xtlrbc,xlrkb->xtlrkc", latent_grads, select, precision=lax.Precision.HIGHEST)
    code_grad = packed.reshape(TOKENS, L, NREG, KR * BLOCK).astype(jnp.bfloat16)
    return (recon_error, decoder_grad, code_grad)
```

```python
import functools

import jax
import jax.numpy as jnp
from jax import lax
from jax.experimental import pallas as pl
from jax.experimental.pallas import tpu as pltpu
from jax.sharding import PartitionSpec as P

BLOCK = 64
PAIR = 2 * BLOCK
VMEM_LIMIT = 40 * 2**20


def params(dims):
    return pltpu.CompilerParams(
        dimension_semantics=("arbitrary",) * dims, vmem_limit_bytes=VMEM_LIMIT
    )


def cost(flops, read):
    return pl.CostEstimate(flops=flops, bytes_accessed=read, transcendentals=0)


def pick_blocks(read_pair, write_pair, index, dup, sources, dests, rows):
    low = lax.broadcasted_iota(jnp.int32, (rows, PAIR), 1) < BLOCK
    for j in range(sources // 2):
        value = read_pair(j)
        turned = pltpu.roll(value, BLOCK, 1)
        dup[2 * j] = jnp.where(low, value, turned)
        dup[2 * j + 1] = jnp.where(low, turned, value)
    dup[sources] = jnp.zeros((rows, PAIR), jnp.float32)
    for j in range(dests // 2):
        write_pair(j, jnp.where(low, dup[index(2 * j)], dup[index(2 * j + 1)]))


def expand_kernel(rows, slots, blocks, inverse, order, src, out, dup):
    step = pl.program_id(0)
    regions = src.shape[1]
    tiles = src.shape[2] // rows
    first = order[step] * tiles
    width = blocks * BLOCK
    for r in range(regions):
        for x in range(tiles):
            here = pl.ds(x * rows, rows)
            base = ((first + x) * regions + r) * blocks

            def read(j):
                return src[0, r, here, pl.ds(j * PAIR, PAIR)].astype(jnp.float32)

            def write(j, value):
                out[here, pl.ds(r * width + j * PAIR, PAIR)] = value.astype(out.dtype)

            pick_blocks(read, write, lambda k: inverse[base + k], dup.at[r * tiles + x], slots, blocks, rows)


def expand(shards, inverse, order, rows, blocks):
    count, regions, own, slot_width = shards.shape
    slots = slot_width // BLOCK
    width = regions * blocks * BLOCK
    return pl.pallas_call(
        functools.partial(expand_kernel, rows, slots, blocks),
        grid_spec=pltpu.PrefetchScalarGridSpec(
            num_scalar_prefetch=2,
            grid=(count,),
            in_specs=[pl.BlockSpec((1, regions, own, slot_width), lambda k, inv, order: (k, 0, 0, 0))],
            out_specs=pl.BlockSpec((own, width), lambda k, inv, order: (order[k], 0)),
            scratch_shapes=[pltpu.VMEM((regions * own // rows, slots + 1, rows, PAIR), jnp.float32)],
        ),
        out_shape=jax.ShapeDtypeStruct((count * own, width), jnp.bfloat16),
        compiler_params=params(1),
        cost_estimate=cost(0, 6 * count * own * width),
        name="expand",
    )(inverse, order, shards)


def rebuild_kernel(codes, dec, *rest):
    out = rest[-1]
    total = jnp.dot(codes[...], dec[0], preferred_element_type=jnp.float32)
    if len(rest) == 2:
        total = total + rest[0][...]
    out[...] = total.astype(out.dtype)


def rebuild(codes, decoder, pair, before, dtype):
    tokens, latents = codes.shape
    columns = decoder.shape[2]
    wide = min(512, columns)
    tile = pl.BlockSpec((tokens, wide), lambda j: (0, j))
    ins = [codes, decoder] + ([] if before is None else [before])
    return pl.pallas_call(
        rebuild_kernel,
        grid=(columns // wide,),
        in_specs=[
            pl.BlockSpec((tokens, latents), lambda j: (0, 0)),
            pl.BlockSpec((1, latents, wide), lambda j: (pair, 0, j)),
        ] + [tile] * (len(ins) - 2),
        out_specs=tile,
        out_shape=jax.ShapeDtypeStruct((tokens, columns), dtype),
        compiler_params=params(1),
        cost_estimate=cost(2 * tokens * latents * columns, 2 * latents * columns),
        name="rebuild",
    )(*ins)


def outer_kernel(codes, error, *rest):
    out = rest[-1]
    out[0] = lax.dot_general(
        codes[...], error[...], (((0,), (0,)), ((), ())), preferred_element_type=jnp.float32
    ).astype(out.dtype)


def outer(codes, error, pair, pairs, held):
    tokens, latents = codes.shape
    columns = error.shape[1]
    high = min(512, latents)
    ins = [codes, error] + ([] if held is None else [held])
    return pl.pallas_call(
        outer_kernel,
        grid=(latents // high,),
        in_specs=[
            pl.BlockSpec((tokens, high), lambda i: (0, i)),
            pl.BlockSpec((tokens, columns), lambda i: (0, 0)),
        ] + [pl.BlockSpec(memory_space=pl.ANY)] * (len(ins) - 2),
        out_specs=pl.BlockSpec((1, high, columns), lambda i: (pair, i, 0)),
        out_shape=jax.ShapeDtypeStruct((pairs, latents, columns), jnp.bfloat16),
        input_output_aliases={} if held is None else {2: 0},
        compiler_params=params(1),
        cost_estimate=cost(2 * tokens * latents * columns, 2 * latents * columns),
        name="outer",
    )(*ins)


def back_kernel(error, dec, out):
    out[...] = lax.dot_general(
        error[...], dec[0], (((1,), (1,)), ((), ())), preferred_element_type=jnp.float32
    )


def back(error, decoder, pair, region_width):
    tokens, columns = error.shape
    latents = decoder.shape[1]
    return pl.pallas_call(
        back_kernel,
        grid=(latents // region_width,),
        in_specs=[
            pl.BlockSpec((tokens, columns), lambda r: (0, 0)),
            pl.BlockSpec((1, region_width, columns), lambda r: (pair, r, 0)),
        ],
        out_specs=pl.BlockSpec((tokens, region_width), lambda r: (0, r)),
        out_shape=jax.ShapeDtypeStruct((tokens, latents), jnp.float32),
        compiler_params=params(1),
        cost_estimate=cost(2 * tokens * latents * columns, 2 * latents * columns),
        name="back",
    )(error, decoder)


def back_compact_kernel(rows, slots, blocks, regions, chosen, error, dec, *rest):
    out, total, dup = rest[-3:]
    r = pl.program_id(0)
    total[...] = lax.dot_general(
        error[...], dec[0], (((1,), (1,)), ((), ())), preferred_element_type=jnp.float32
    )
    for x in range(total.shape[0] // rows):
        here = pl.ds(x * rows, rows)
        base = (x * regions + r) * slots

        def read(j):
            value = total[here, pl.ds(j * PAIR, PAIR)]
            if len(rest) == 4:
                value = value + rest[0][here, pl.ds(j * PAIR, PAIR)]
            return value

        def write(j, value):
            out[0, here, pl.ds(j * PAIR, PAIR)] = value.astype(out.dtype)

        pick_blocks(read, write, lambda k: chosen[base + k], dup.at[x % 4], blocks, slots, rows)


def back_compact(error, decoder, pair, before, chosen, rows, slots, regions):
    tokens, columns = error.shape
    latents = decoder.shape[1]
    width = latents // regions
    blocks = width // BLOCK
    ins = [error, decoder] + ([] if before is None else [before])
    return pl.pallas_call(
        functools.partial(back_compact_kernel, rows, slots, blocks, regions),
        grid_spec=pltpu.PrefetchScalarGridSpec(
            num_scalar_prefetch=1,
            grid=(regions,),
            in_specs=[
                pl.BlockSpec((tokens, columns), lambda r, ch: (0, 0)),
                pl.BlockSpec((1, width, columns), lambda r, ch: (pair, r, 0)),
            ] + [pl.BlockSpec((tokens, width), lambda r, ch: (0, r))] * (len(ins) - 2),
            out_specs=pl.BlockSpec((1, tokens, slots * BLOCK), lambda r, ch: (r, 0, 0)),
            scratch_shapes=[
                pltpu.VMEM((tokens, width), jnp.float32),
                pltpu.VMEM((4, blocks + 1, rows, PAIR), jnp.float32),
            ],
        ),
        out_shape=jax.ShapeDtypeStruct((regions, tokens, slots * BLOCK), jnp.bfloat16),
        compiler_params=params(1),
        cost_estimate=cost(2 * tokens * latents * columns, 2 * latents * columns),
        name="back_compact",
    )(chosen, *ins)


def gather_tok(own):
    count = lax.axis_size("tok")
    me = lax.axis_index("tok")
    up, down = [own], [own]
    for m in range(1, count):
        up.append(lax.ppermute(up[-1], "tok", [(i, i + 1) for i in range(m - 1, count - 1)]))
        down.append(lax.ppermute(down[-1], "tok", [(i, i - 1) for i in range(1, count - m + 1)]))
    return jnp.stack([own] + [jnp.where(me >= k, up[k], down[count - k]) for k in range(1, count)])


def reduce_tok(parts):
    count = lax.axis_size("tok")
    me = lax.axis_index("tok")

    def chunk(d):
        return lax.dynamic_index_in_dim(parts, d, 1, keepdims=False).astype(jnp.float32)

    own = chunk(me)
    flows = []
    for sign in (1, -1):
        got = None
        for m in range(1, count):
            if sign > 0:
                owner = jnp.minimum(count - m + me, count - 1)
                perm = [(i, i + 1) for i in range(min(m, count - 1))]
            else:
                owner = jnp.maximum(me - (count - m), 0)
                perm = [(count - 1 - i, count - 2 - i) for i in range(min(m, count - 1))]
            send = chunk(owner)
            if got is not None:
                send = send + got.astype(jnp.float32)
            got = lax.ppermute(send.astype(jnp.bfloat16), "tok", perm)
        flows.append(got.astype(jnp.float32))
    return (own + flows[0] + flows[1]).astype(jnp.bfloat16)


def core_swap(value):
    count = lax.axis_size("blk")
    return lax.ppermute(value, "blk", [(i, i ^ 1) for i in range(count)])


def row_shift(value, k):
    count = lax.axis_size("blk")
    return lax.ppermute(value, "blk", [(i, (i + 2 * k) % count) for i in range(count)])


def reduce_blk(part):
    count = lax.axis_size("blk")
    me = lax.axis_index("blk")
    core, row, chips = me % 2, me // 2, count // 2
    tokens, columns = part.shape
    split = part.reshape(chips, 2, tokens // count, columns)
    send = lax.dynamic_index_in_dim(split, 1 - core, 1, keepdims=False)
    kept = lax.dynamic_index_in_dim(split, core, 1, keepdims=False)
    both = kept.astype(jnp.float32) + core_swap(send).astype(jnp.float32)

    def shard(r):
        return lax.dynamic_index_in_dim(both, r, 0, keepdims=False)

    total = shard(row)
    for k in range(1, chips):
        sent = shard((row + k) % chips).astype(jnp.bfloat16)
        total = total + row_shift(sent, k).astype(jnp.float32)
    return total


def gather_blk(own):
    count = lax.axis_size("blk")
    me = lax.axis_index("blk")
    core, row, chips = me % 2, me // 2, count // 2
    held = [own] + [row_shift(own, k) for k in range(1, chips)]
    mine = []
    for r in range(chips):
        value = held[0]
        for k in range(1, chips):
            value = jnp.where((row - k + chips) % chips == r, held[k], value)
        mine.append(value)
    mine = jnp.stack(mine)
    other = core_swap(mine)
    even = jnp.where(core == 0, mine, other)
    odd = jnp.where(core == 0, other, mine)
    return jnp.stack([even, odd], 1).reshape(count * own.shape[0], own.shape[1])


def per_device(latent_codes, block_lists, block_counts, decoder, targets):
    own_rows, layers, regions, slot_width = latent_codes.shape
    slots = block_lists.shape[3]
    latents = decoder.shape[1]
    region_width = latents // regions
    blocks = region_width // BLOCK
    count = lax.axis_size("tok")
    tokens = count * own_rows
    rows = tokens // block_lists.shape[0]
    me = lax.axis_index("tok")

    own = latent_codes.transpose(1, 2, 0, 3)
    gathered = [gather_tok(own[s]) for s in range(layers)]

    active = lax.broadcasted_iota(jnp.int32, block_lists.shape, 3) < block_counts[..., None]
    chosen = jnp.where(active, block_lists, blocks)
    slot = lax.broadcasted_iota(jnp.int32, block_lists.shape + (blocks,), 3)
    block = lax.broadcasted_iota(jnp.int32, block_lists.shape + (blocks,), 4)
    inverse = jnp.min(jnp.where(chosen[..., None] == block, slot, slots), axis=3)
    order = (me - jnp.arange(count, dtype=jnp.int32) + count) % count

    codes = [
        expand(gathered[s], inverse[:, s].reshape(-1), order, rows, blocks) for s in range(layers)
    ]

    part0 = rebuild(codes[0], decoder, 0, None, jnp.bfloat16)
    partial = rebuild(codes[0], decoder, 1, None, jnp.float32)
    part1 = rebuild(codes[1], decoder, 2, partial, jnp.bfloat16)

    def error_of(part, t):
        return (reduce_blk(part) - targets[:, t].astype(jnp.float32)).astype(jnp.bfloat16)

    own_error = [error_of(part0, 0), error_of(part1, 1)]
    recon_error = jnp.stack(own_error, 1)
    error = [gather_blk(e) for e in own_error]

    grads = outer(codes[0], error[0], 0, decoder.shape[0], None)
    early = back(error[0], decoder, 0, region_width)

    def codes_grad(t, pair, before, s):
        packed = back_compact(
            error[t], decoder, pair, before, chosen[:, s].reshape(-1), rows, slots, regions
        )
        return reduce_tok(packed.reshape(regions, count, own_rows, slot_width))

    grad1 = codes_grad(1, 2, None, 1)
    grad0 = codes_grad(1, 1, early, 0)
    grads = outer(codes[0], error[1], 1, decoder.shape[0], grads)
    grads = outer(codes[1], error[1], 2, decoder.shape[0], grads)
    code_grad = jnp.stack([grad0, grad1], 0).transpose(2, 0, 1, 3)
    return (recon_error, grads, code_grad)


def solution(mesh):
    placed = (
        P(("groups", "tok"), None, "blk", None),
        P("groups", None, "blk", None),
        P("groups", None, "blk"),
        P(None, "blk", "tok"),
        P(("groups", "blk"), None, "tok"),
    )
    return jax.shard_map(
        per_device,
        mesh=mesh,
        in_specs=placed,
        out_specs=(
            P(("groups", "blk"), None, "tok"),
            P("groups", "blk", "tok"),
            P(("groups", "tok"), None, "blk", None),
        ),
        check_vma=False,
    )
```

```python
import functools

import jax
import jax.numpy as jnp
from jax import lax
from jax.experimental import pallas as pl
from jax.experimental.pallas import tpu as pltpu
from jax.sharding import PartitionSpec as P

BLOCK = 64
PAIR = 2 * BLOCK
VMEM_LIMIT = 48 * 2**20


def params(dims):
    return pltpu.CompilerParams(
        dimension_semantics=("arbitrary",) * dims if dims else None, vmem_limit_bytes=VMEM_LIMIT
    )


def cost(flops, read):
    return pl.CostEstimate(flops=flops, bytes_accessed=read, transcendentals=0)


def pick_blocks(read_pair, write_pair, index, dup, sources, dests, rows):
    low = lax.broadcasted_iota(jnp.int32, (rows, PAIR), 1) < BLOCK
    for j in range(sources // 2):
        value = read_pair(j)
        turned = pltpu.roll(value, BLOCK, 1)
        dup[2 * j] = jnp.where(low, value, turned)
        dup[2 * j + 1] = jnp.where(low, turned, value)
    dup[sources] = jnp.zeros((rows, PAIR), jnp.float32)
    for j in range(dests // 2):
        write_pair(j, jnp.where(low, dup[index(2 * j)], dup[index(2 * j + 1)]))


def expand_kernel(rows, slots, blocks, inverse, order, src, out, dup):
    step = pl.program_id(0)
    regions = src.shape[1]
    tiles = src.shape[2] // rows
    first = order[step] * tiles
    width = blocks * BLOCK
    for r in range(regions):
        for x in range(tiles):
            here = pl.ds(x * rows, rows)
            base = ((first + x) * regions + r) * blocks

            def read(j):
                return src[0, r, here, pl.ds(j * PAIR, PAIR)].astype(jnp.float32)

            def write(j, value):
                out[here, pl.ds(r * width + j * PAIR, PAIR)] = value.astype(out.dtype)

            pick_blocks(read, write, lambda k: inverse[base + k], dup.at[r * tiles + x], slots, blocks, rows)


def expand(shards, inverse, order, rows, blocks):
    count, regions, own, slot_width = shards.shape
    slots = slot_width // BLOCK
    width = regions * blocks * BLOCK
    return pl.pallas_call(
        functools.partial(expand_kernel, rows, slots, blocks),
        grid_spec=pltpu.PrefetchScalarGridSpec(
            num_scalar_prefetch=2,
            grid=(count,),
            in_specs=[pl.BlockSpec((1, regions, own, slot_width), lambda k, inv, order: (k, 0, 0, 0))],
            out_specs=pl.BlockSpec((own, width), lambda k, inv, order: (order[k], 0)),
            scratch_shapes=[pltpu.VMEM((regions * own // rows, slots + 1, rows, PAIR), jnp.float32)],
        ),
        out_shape=jax.ShapeDtypeStruct((count * own, width), jnp.bfloat16),
        compiler_params=params(1),
        cost_estimate=cost(0, 6 * count * own * width),
        name="expand",
    )(inverse, order, shards)


DEPTH = 4


def stream(copies, work):
    count = len(copies)
    for i in range(min(DEPTH, count)):
        copies[i].start()
    for i in range(count):
        copies[i].wait()
        if i + DEPTH < count:
            copies[i + DEPTH].start()
        work(i)


def rebuild_kernel(pair, codes, dec, *rest):
    out, held, sems = rest[-3:]
    wide = held.shape[2]

    def work(i):
        here = pl.ds(i * wide, wide)
        total = jnp.dot(codes[...], held[i], preferred_element_type=jnp.float32)
        if len(rest) == 4:
            total = total + rest[0][:, here]
        out[:, here] = total.astype(out.dtype)

    stream(
        [
            pltpu.make_async_copy(dec.at[pair, :, pl.ds(i * wide, wide)], held.at[i], sems.at[i])
            for i in range(held.shape[0])
        ],
        work,
    )


def rebuild(codes, decoder, pair, before, dtype):
    tokens, latents = codes.shape
    columns = decoder.shape[2]
    wide = min(256, columns)
    whole = pl.BlockSpec(memory_space=pltpu.VMEM)
    ins = [codes, decoder] + ([] if before is None else [before])
    return pl.pallas_call(
        functools.partial(rebuild_kernel, pair),
        in_specs=[whole, pl.BlockSpec(memory_space=pl.ANY)] + [whole] * (len(ins) - 2),
        out_specs=whole,
        out_shape=jax.ShapeDtypeStruct((tokens, columns), dtype),
        scratch_shapes=[
            pltpu.VMEM((columns // wide, latents, wide), jnp.bfloat16),
            pltpu.SemaphoreType.DMA((columns // wide,)),
        ],
        compiler_params=params(0),
        cost_estimate=cost(2 * tokens * latents * columns, 2 * latents * columns),
        name="rebuild",
    )(*ins)


def outer_kernel(pair, codes, error, *rest):
    out, held, sems = rest[-3:]
    high = held.shape[1]
    copies = []
    for i in range(held.shape[0]):
        here = pl.ds(i * high, high)
        held[i] = lax.dot_general(
            codes[:, here], error[...], (((0,), (0,)), ((), ())), preferred_element_type=jnp.float32
        ).astype(out.dtype)
        copies.append(pltpu.make_async_copy(held.at[i], out.at[pair, here], sems.at[i]))
        copies[-1].start()
    for copy in copies:
        copy.wait()


def outer(codes, error, pair, pairs, held):
    tokens, latents = codes.shape
    columns = error.shape[1]
    high = min(512, latents)
    whole = pl.BlockSpec(memory_space=pltpu.VMEM)
    far = pl.BlockSpec(memory_space=pl.ANY)
    ins = [codes, error] + ([] if held is None else [held])
    return pl.pallas_call(
        functools.partial(outer_kernel, pair),
        in_specs=[whole, whole] + [far] * (len(ins) - 2),
        out_specs=far,
        out_shape=jax.ShapeDtypeStruct((pairs, latents, columns), jnp.bfloat16),
        input_output_aliases={} if held is None else {2: 0},
        scratch_shapes=[
            pltpu.VMEM((latents // high, high, columns), jnp.bfloat16),
            pltpu.SemaphoreType.DMA((latents // high,)),
        ],
        compiler_params=params(0),
        cost_estimate=cost(2 * tokens * latents * columns, 2 * latents * columns),
        name="outer",
    )(*ins)


def back_compact_kernel(rows, slots, blocks, regions, pairs, chosen, *rest):
    errors, (dec, out, total, dup, held, sems) = rest[: len(pairs)], rest[len(pairs):]
    high = held.shape[1]
    width = blocks * BLOCK
    parts = width // high

    def finish(r):
        for x in range(total.shape[1] // rows):
            here = pl.ds(x * rows, rows)
            base = (x * regions + r) * slots

            def read(j):
                return total[r % 2, here, pl.ds(j * PAIR, PAIR)]

            def write(j, value):
                out[r, here, pl.ds(j * PAIR, PAIR)] = value.astype(out.dtype)

            pick_blocks(read, write, lambda k: chosen[base + k], dup.at[x % 4], blocks, slots, rows)

    def work(i):
        step, which = i // len(pairs), i % len(pairs)
        r, here = step // parts, pl.ds(step % parts * high, high)
        value = lax.dot_general(
            errors[which][...], held[i], (((1,), (1,)), ((), ())), preferred_element_type=jnp.float32
        )
        if which > 0:
            value = value + total[r % 2, :, here]
        total[r % 2, :, here] = value
        if step % parts == parts - 1 and which == len(pairs) - 1:
            finish(r)

    stream(
        [
            pltpu.make_async_copy(
                dec.at[pairs[i % len(pairs)], pl.ds(i // len(pairs) * high, high)], held.at[i], sems.at[i]
            )
            for i in range(held.shape[0])
        ],
        work,
    )


def back_compact(errors, decoder, pairs, chosen, rows, slots, regions):
    tokens, columns = errors[0].shape
    latents = decoder.shape[1]
    width = latents // regions
    blocks = width // BLOCK
    high = min(512, width)
    steps = latents // high * len(pairs)
    whole = pl.BlockSpec(memory_space=pltpu.VMEM)
    return pl.pallas_call(
        functools.partial(back_compact_kernel, rows, slots, blocks, regions, pairs),
        in_specs=[pl.BlockSpec(memory_space=pltpu.SMEM)]
        + [whole] * len(pairs)
        + [pl.BlockSpec(memory_space=pl.ANY)],
        out_specs=whole,
        out_shape=jax.ShapeDtypeStruct((regions, tokens, slots * BLOCK), jnp.bfloat16),
        scratch_shapes=[
            pltpu.VMEM((2, tokens, width), jnp.float32),
            pltpu.VMEM((4, blocks + 1, rows, PAIR), jnp.float32),
            pltpu.VMEM((steps, high, columns), jnp.bfloat16),
            pltpu.SemaphoreType.DMA((steps,)),
        ],
        compiler_params=params(0),
        cost_estimate=cost(
            2 * len(pairs) * tokens * latents * columns, 2 * len(pairs) * latents * columns
        ),
        name="back_compact",
    )(chosen, *errors, decoder)


def tok_shift(value, k):
    count = lax.axis_size("tok")
    return lax.ppermute(value, "tok", [(i, (i + k) % count) for i in range(count)])


def gather_tok(own):
    count = lax.axis_size("tok")
    return jnp.stack([own] + [tok_shift(own, k) for k in range(1, count)])


def reduce_tok(parts):
    count = lax.axis_size("tok")
    me = lax.axis_index("tok")

    def chunk(k):
        return lax.dynamic_index_in_dim(parts, (me + k) % count, 1, keepdims=False)

    got = [tok_shift(chunk(k), k) for k in range(1, count)]
    total = chunk(0).astype(jnp.float32)
    for value in got:
        total = total + value.astype(jnp.float32)
    return total.astype(jnp.bfloat16)


def core_swap(value):
    count = lax.axis_size("blk")
    return lax.ppermute(value, "blk", [(i, i ^ 1) for i in range(count)])


def row_shift(value, k):
    count = lax.axis_size("blk")
    return lax.ppermute(value, "blk", [(i, (i + 2 * k) % count) for i in range(count)])


def reduce_blk(part):
    count = lax.axis_size("blk")
    me = lax.axis_index("blk")
    core, row, chips = me % 2, me // 2, count // 2
    tokens, columns = part.shape
    split = part.reshape(chips, 2, tokens // count, columns)
    send = lax.dynamic_index_in_dim(split, 1 - core, 1, keepdims=False)
    kept = lax.dynamic_index_in_dim(split, core, 1, keepdims=False)
    both = kept.astype(jnp.float32) + core_swap(send).astype(jnp.float32)

    def shard(r):
        return lax.dynamic_index_in_dim(both, r, 0, keepdims=False)

    total = shard(row)
    for k in range(1, chips):
        sent = shard((row + k) % chips).astype(jnp.bfloat16)
        total = total + row_shift(sent, k).astype(jnp.float32)
    return total


def gather_blk(own):
    count = lax.axis_size("blk")
    me = lax.axis_index("blk")
    core, row, chips = me % 2, me // 2, count // 2
    held = [own] + [row_shift(own, k) for k in range(1, chips)]
    mine = []
    for r in range(chips):
        value = held[0]
        for k in range(1, chips):
            value = jnp.where((row - k + chips) % chips == r, held[k], value)
        mine.append(value)
    mine = jnp.stack(mine)
    other = core_swap(mine)
    even = jnp.where(core == 0, mine, other)
    odd = jnp.where(core == 0, other, mine)
    return jnp.stack([even, odd], 1).reshape(count * own.shape[0], own.shape[1])


def per_device(latent_codes, block_lists, block_counts, decoder, targets):
    own_rows, layers, regions, slot_width = latent_codes.shape
    slots = block_lists.shape[3]
    latents = decoder.shape[1]
    region_width = latents // regions
    blocks = region_width // BLOCK
    count = lax.axis_size("tok")
    tokens = count * own_rows
    rows = tokens // block_lists.shape[0]
    me = lax.axis_index("tok")

    own = latent_codes.transpose(1, 2, 0, 3)
    gathered0 = gather_tok(own[0])
    gathered0, own1 = lax.optimization_barrier((gathered0, own[1]))
    gathered = [gathered0, gather_tok(own1)]

    active = lax.broadcasted_iota(jnp.int32, block_lists.shape, 3) < block_counts[..., None]
    chosen = jnp.where(active, block_lists, blocks)
    slot = lax.broadcasted_iota(jnp.int32, block_lists.shape + (blocks,), 3)
    block = lax.broadcasted_iota(jnp.int32, block_lists.shape + (blocks,), 4)
    inverse = jnp.min(jnp.where(chosen[..., None] == block, slot, slots), axis=3)
    order = (me - jnp.arange(count, dtype=jnp.int32) + count) % count

    codes = [
        expand(gathered[s], inverse[:, s].reshape(-1), order, rows, blocks) for s in range(layers)
    ]

    part0 = rebuild(codes[0], decoder, 0, None, jnp.bfloat16)
    part0, codes0 = lax.optimization_barrier((part0, codes[0]))
    partial = rebuild(codes0, decoder, 1, None, jnp.float32)
    part1 = rebuild(codes[1], decoder, 2, partial, jnp.bfloat16)

    def error_of(part, t):
        return (reduce_blk(part) - targets[:, t].astype(jnp.float32)).astype(jnp.bfloat16)

    own_error = [error_of(part0, 0), error_of(part1, 1)]
    recon_error = jnp.stack(own_error, 1)
    error = [gather_blk(e) for e in own_error]

    grads = outer(codes[0], error[0], 0, decoder.shape[0], None)

    def codes_grad(errors, pairs, s):
        packed = back_compact(
            errors, decoder, pairs, chosen[:, s].reshape(-1), rows, slots, regions
        )
        return reduce_tok(packed.reshape(regions, count, own_rows, slot_width))

    grad1 = codes_grad([error[1]], [2], 1)
    grad0 = codes_grad(error, [0, 1], 0)
    grads = outer(codes[0], error[1], 1, decoder.shape[0], grads)
    grads = outer(codes[1], error[1], 2, decoder.shape[0], grads)
    code_grad = jnp.stack([grad0, grad1], 0).transpose(2, 0, 1, 3)
    return (recon_error, grads, code_grad)


def solution(mesh):
    placed = (
        P(("groups", "tok"), None, "blk", None),
        P("groups", None, "blk", None),
        P("groups", None, "blk"),
        P(None, "blk", "tok"),
        P(("groups", "blk"), None, "tok"),
    )
    return jax.shard_map(
        per_device,
        mesh=mesh,
        in_specs=placed,
        out_specs=(
            P(("groups", "blk"), None, "tok"),
            P("groups", "blk", "tok"),
            P(("groups", "tok"), None, "blk", None),
        ),
        check_vma=False,
    )
```

```python
import functools

import jax
import jax.numpy as jnp
from jax import lax
from jax.experimental import pallas as pl
from jax.experimental.pallas import tpu as pltpu
from jax.sharding import PartitionSpec as P

BLOCK = 64
PAIR = 2 * BLOCK
VMEM_LIMIT = 48 * 2**20


def params(dims):
    return pltpu.CompilerParams(
        dimension_semantics=("arbitrary",) * dims if dims else None, vmem_limit_bytes=VMEM_LIMIT
    )


def cost(flops, read, scale=1):
    return pl.CostEstimate(
        flops=flops // scale, bytes_accessed=read // scale, transcendentals=0
    )


def pick_blocks(read_pair, write_pair, index, dup, sources, dests, rows):
    low = lax.broadcasted_iota(jnp.int32, (rows, PAIR), 1) < BLOCK
    for j in range(sources // 2):
        value = read_pair(j)
        turned = pltpu.roll(value, BLOCK, 1)
        dup[2 * j] = jnp.where(low, value, turned)
        dup[2 * j + 1] = jnp.where(low, turned, value)
    dup[sources] = jnp.zeros((rows, PAIR), jnp.float32)
    for j in range(dests // 2):
        write_pair(j, jnp.where(low, dup[index(2 * j)], dup[index(2 * j + 1)]))


def expand_kernel(rows, slots, blocks, inverse, order, src, out, dup):
    step = pl.program_id(0)
    regions = src.shape[1]
    tiles = src.shape[2] // rows
    first = order[step] * tiles
    width = blocks * BLOCK
    for r in range(regions):
        for x in range(tiles):
            here = pl.ds(x * rows, rows)
            base = ((first + x) * regions + r) * blocks

            def read(j):
                return src[0, r, here, pl.ds(j * PAIR, PAIR)].astype(jnp.float32)

            def write(j, value):
                out[here, pl.ds(r * width + j * PAIR, PAIR)] = value.astype(out.dtype)

            pick_blocks(read, write, lambda k: inverse[base + k], dup.at[r * tiles + x], slots, blocks, rows)


def expand(shards, inverse, order, rows, blocks):
    count, regions, own, slot_width = shards.shape
    slots = slot_width // BLOCK
    width = regions * blocks * BLOCK
    return pl.pallas_call(
        functools.partial(expand_kernel, rows, slots, blocks),
        grid_spec=pltpu.PrefetchScalarGridSpec(
            num_scalar_prefetch=2,
            grid=(count,),
            in_specs=[pl.BlockSpec((1, regions, own, slot_width), lambda k, inv, order: (k, 0, 0, 0))],
            out_specs=pl.BlockSpec((own, width), lambda k, inv, order: (order[k], 0)),
            scratch_shapes=[pltpu.VMEM((regions * own // rows, slots + 1, rows, PAIR), jnp.float32)],
        ),
        out_shape=jax.ShapeDtypeStruct((count * own, width), jnp.bfloat16),
        compiler_params=params(1),
        cost_estimate=cost(0, 6 * count * own * width),
        name="expand",
    )(inverse, order, shards)


DEPTH = 4


def stream(copies, work):
    count = len(copies)
    for i in range(min(DEPTH, count)):
        copies[i].start()
    for i in range(count):
        copies[i].wait()
        if i + DEPTH < count:
            copies[i + DEPTH].start()
        work(i)


def rebuild_kernel(pair, codes, dec, *rest):
    out, total, held, sems = rest[-4:]
    high = held.shape[1]
    count = held.shape[0]

    def work(i):
        value = jnp.dot(
            codes[:, pl.ds(i * high, high)], held[i], preferred_element_type=jnp.float32
        )
        if i > 0:
            value = value + total[...]
        elif len(rest) == 5:
            value = value + rest[0][...]
        if i < count - 1:
            total[...] = value
        else:
            out[...] = value.astype(out.dtype)

    stream(
        [
            pltpu.make_async_copy(dec.at[pair, pl.ds(i * high, high)], held.at[i], sems.at[i])
            for i in range(count)
        ],
        work,
    )


def rebuild(codes, decoder, pair, before, dtype):
    tokens, latents = codes.shape
    columns = decoder.shape[2]
    high = min(512, latents)
    whole = pl.BlockSpec(memory_space=pltpu.VMEM)
    ins = [codes, decoder] + ([] if before is None else [before])
    return pl.pallas_call(
        functools.partial(rebuild_kernel, pair),
        in_specs=[whole, pl.BlockSpec(memory_space=pl.ANY)] + [whole] * (len(ins) - 2),
        out_specs=whole,
        out_shape=jax.ShapeDtypeStruct((tokens, columns), dtype),
        scratch_shapes=[
            pltpu.VMEM((tokens, columns), jnp.float32),
            pltpu.VMEM((latents // high, high, columns), jnp.bfloat16),
            pltpu.SemaphoreType.DMA((latents // high,)),
        ],
        compiler_params=params(0),
        cost_estimate=cost(2 * tokens * latents * columns, 2 * latents * columns),
        name="rebuild",
    )(*ins)


def outer_kernel(pair, codes, error, *rest):
    out, held, sems = rest[-3:]
    high = held.shape[1]
    copies = []
    for i in range(held.shape[0]):
        here = pl.ds(i * high, high)
        held[i] = lax.dot_general(
            codes[:, here], error[...], (((0,), (0,)), ((), ())), preferred_element_type=jnp.float32
        ).astype(out.dtype)
        copies.append(pltpu.make_async_copy(held.at[i], out.at[pair, here], sems.at[i]))
        copies[-1].start()
    for copy in copies:
        copy.wait()


def outer(codes, error, pair, pairs, held):
    tokens, latents = codes.shape
    columns = error.shape[1]
    high = min(512, latents)
    whole = pl.BlockSpec(memory_space=pltpu.VMEM)
    far = pl.BlockSpec(memory_space=pl.ANY)
    ins = [codes, error] + ([] if held is None else [held])
    return pl.pallas_call(
        functools.partial(outer_kernel, pair),
        in_specs=[whole, whole] + [far] * (len(ins) - 2),
        out_specs=far,
        out_shape=jax.ShapeDtypeStruct((pairs, latents, columns), jnp.bfloat16),
        input_output_aliases={} if held is None else {2: 0},
        scratch_shapes=[
            pltpu.VMEM((latents // high, high, columns), jnp.bfloat16),
            pltpu.SemaphoreType.DMA((latents // high,)),
        ],
        compiler_params=params(0),
        cost_estimate=cost(2 * tokens * latents * columns, 2 * latents * columns),
        name="outer",
    )(*ins)


def back_compact_kernel(rows, slots, blocks, regions, pairs, chosen, *rest):
    errors, (dec, out, total, dup, held, sems) = rest[: len(pairs)], rest[len(pairs):]
    high = held.shape[1]
    width = blocks * BLOCK
    parts = width // high

    def finish(r):
        for x in range(total.shape[1] // rows):
            here = pl.ds(x * rows, rows)
            base = (x * regions + r) * slots

            def read(j):
                return total[r % 2, here, pl.ds(j * PAIR, PAIR)]

            def write(j, value):
                out[r, here, pl.ds(j * PAIR, PAIR)] = value.astype(out.dtype)

            pick_blocks(read, write, lambda k: chosen[base + k], dup.at[x % 4], blocks, slots, rows)

    def work(i):
        step, which = i // len(pairs), i % len(pairs)
        r, here = step // parts, pl.ds(step % parts * high, high)
        value = lax.dot_general(
            errors[which][...], held[i], (((1,), (1,)), ((), ())), preferred_element_type=jnp.float32
        )
        if which > 0:
            value = value + total[r % 2, :, here]
        total[r % 2, :, here] = value
        if step % parts == parts - 1 and which == len(pairs) - 1:
            finish(r)

    stream(
        [
            pltpu.make_async_copy(
                dec.at[pairs[i % len(pairs)], pl.ds(i // len(pairs) * high, high)], held.at[i], sems.at[i]
            )
            for i in range(held.shape[0])
        ],
        work,
    )


def back_compact(errors, decoder, pairs, chosen, rows, slots, regions):
    tokens, columns = errors[0].shape
    latents = decoder.shape[1]
    width = latents // regions
    blocks = width // BLOCK
    high = min(512, width)
    steps = latents // high * len(pairs)
    whole = pl.BlockSpec(memory_space=pltpu.VMEM)
    return pl.pallas_call(
        functools.partial(back_compact_kernel, rows, slots, blocks, regions, pairs),
        in_specs=[pl.BlockSpec(memory_space=pltpu.SMEM)]
        + [whole] * len(pairs)
        + [pl.BlockSpec(memory_space=pl.ANY)],
        out_specs=whole,
        out_shape=jax.ShapeDtypeStruct((regions, tokens, slots * BLOCK), jnp.bfloat16),
        scratch_shapes=[
            pltpu.VMEM((2, tokens, width), jnp.float32),
            pltpu.VMEM((4, blocks + 1, rows, PAIR), jnp.float32),
            pltpu.VMEM((steps, high, columns), jnp.bfloat16),
            pltpu.SemaphoreType.DMA((steps,)),
        ],
        compiler_params=params(0),
        cost_estimate=cost(
            2 * len(pairs) * tokens * latents * columns, 2 * len(pairs) * latents * columns, 16
        ),
        name="back_compact",
    )(chosen, *errors, decoder)


def tok_shift(value, k):
    count = lax.axis_size("tok")
    return lax.ppermute(value, "tok", [(i, (i + k) % count) for i in range(count)])


def gather_tok(own):
    count = lax.axis_size("tok")
    return jnp.stack([own] + [tok_shift(own, k) for k in range(1, count)])


def chunks_tok(parts):
    count = lax.axis_size("tok")
    me = lax.axis_index("tok")
    return [
        lax.dynamic_index_in_dim(parts, (me + k) % count, 1, keepdims=False) for k in range(count)
    ]


def sent_tok(chunks):
    return [tok_shift(chunks[k], k) for k in range(1, len(chunks))]


def sum_tok(chunks, got):
    total = chunks[0].astype(jnp.float32)
    for value in got:
        total = total + value.astype(jnp.float32)
    return total.astype(jnp.bfloat16)


def core_swap(value):
    count = lax.axis_size("blk")
    return lax.ppermute(value, "blk", [(i, i ^ 1) for i in range(count)])


def row_shift(value, k):
    count = lax.axis_size("blk")
    return lax.ppermute(value, "blk", [(i, (i + 2 * k) % count) for i in range(count)])


def reduce_core(part):
    count = lax.axis_size("blk")
    core = lax.axis_index("blk") % 2
    tokens, columns = part.shape
    split = part.reshape(count // 2, 2, tokens // count, columns)
    send = lax.dynamic_index_in_dim(split, 1 - core, 1, keepdims=False)
    kept = lax.dynamic_index_in_dim(split, core, 1, keepdims=False)
    return kept.astype(jnp.float32) + core_swap(send).astype(jnp.float32)


def reduce_row(both):
    row, chips = lax.axis_index("blk") // 2, both.shape[0]

    def shard(r):
        return lax.dynamic_index_in_dim(both, r, 0, keepdims=False)

    total = shard(row)
    for k in range(1, chips):
        sent = shard((row + k) % chips).astype(jnp.bfloat16)
        total = total + row_shift(sent, k).astype(jnp.float32)
    return total


def gather_blk(own):
    count = lax.axis_size("blk")
    me = lax.axis_index("blk")
    core, row, chips = me % 2, me // 2, count // 2
    held = [own] + [row_shift(own, k) for k in range(1, chips)]
    mine = []
    for r in range(chips):
        value = held[0]
        for k in range(1, chips):
            value = jnp.where((row - k + chips) % chips == r, held[k], value)
        mine.append(value)
    mine = jnp.stack(mine)
    other = core_swap(mine)
    even = jnp.where(core == 0, mine, other)
    odd = jnp.where(core == 0, other, mine)
    return jnp.stack([even, odd], 1).reshape(count * own.shape[0], own.shape[1])


def per_device(latent_codes, block_lists, block_counts, decoder, targets):
    own_rows, layers, regions, slot_width = latent_codes.shape
    slots = block_lists.shape[3]
    latents = decoder.shape[1]
    region_width = latents // regions
    blocks = region_width // BLOCK
    count = lax.axis_size("tok")
    tokens = count * own_rows
    rows = tokens // block_lists.shape[0]
    me = lax.axis_index("tok")

    own = latent_codes.transpose(1, 2, 0, 3)
    gathered0 = gather_tok(own[0])
    gathered0, own1 = lax.optimization_barrier((gathered0, own[1]))
    gathered = [gathered0, gather_tok(own1)]

    active = lax.broadcasted_iota(jnp.int32, block_lists.shape, 3) < block_counts[..., None]
    chosen = jnp.where(active, block_lists, blocks)
    slot = lax.broadcasted_iota(jnp.int32, block_lists.shape + (blocks,), 3)
    block = lax.broadcasted_iota(jnp.int32, block_lists.shape + (blocks,), 4)
    inverse = jnp.min(jnp.where(chosen[..., None] == block, slot, slots), axis=3)
    order = (me - jnp.arange(count, dtype=jnp.int32) + count) % count

    def spread(s, shards):
        return expand(shards, inverse[:, s].reshape(-1), order, rows, blocks)

    codes = [spread(0, gathered[0])]
    part0 = rebuild(codes[0], decoder, 0, None, jnp.bfloat16)

    def error_of(both, t):
        return (reduce_row(both) - targets[:, t].astype(jnp.float32)).astype(jnp.bfloat16)

    both0 = reduce_core(part0)
    codes0, both0 = lax.optimization_barrier((codes[0], both0))
    partial = rebuild(codes0, decoder, 1, None, jnp.float32)
    error0 = error_of(both0, 0)
    partial, error0, shards1 = lax.optimization_barrier((partial, error0, gathered[1]))
    codes.append(spread(1, shards1))
    part1 = rebuild(codes[1], decoder, 2, partial, jnp.bfloat16)
    error1 = error_of(reduce_core(part1), 1)
    recon_error = jnp.stack([error0, error1], 1)
    all0 = gather_blk(error0)
    error = [all0, gather_blk(error1)]

    def codes_chunks(errors, pairs, s):
        packed = back_compact(
            errors, decoder, pairs, chosen[:, s].reshape(-1), rows, slots, regions
        )
        return chunks_tok(packed.reshape(regions, count, own_rows, slot_width))

    chunks1 = codes_chunks([error[1]], [2], 1)
    chunks1, after1 = lax.optimization_barrier((chunks1, all0))
    got1 = sent_tok(chunks1)
    grads = outer(codes[0], after1, 0, decoder.shape[0], None)
    grads, got1[0], after1 = lax.optimization_barrier((grads, got1[0], after1))
    chunks0 = codes_chunks([after1, error[1]], [0, 1], 0)
    chunks0, late = lax.optimization_barrier((chunks0, error[1]))
    grad0 = sum_tok(chunks0, sent_tok(chunks0))
    grad1 = sum_tok(chunks1, got1)
    grads = outer(codes[0], late, 1, decoder.shape[0], grads)
    grads = outer(codes[1], late, 2, decoder.shape[0], grads)
    code_grad = jnp.stack([grad0, grad1], 0).transpose(2, 0, 1, 3)
    return (recon_error, grads, code_grad)


def solution(mesh):
    placed = (
        P(("groups", "tok"), None, "blk", None),
        P("groups", None, "blk", None),
        P("groups", None, "blk"),
        P(None, "blk", "tok"),
        P(("groups", "blk"), None, "tok"),
    )
    return jax.shard_map(
        per_device,
        mesh=mesh,
        in_specs=placed,
        out_specs=(
            P(("groups", "blk"), None, "tok"),
            P("groups", "blk", "tok"),
            P(("groups", "tok"), None, "blk", None),
        ),
        check_vma=False,
    )
```
